256 devices in a mesh: dp: 16 (over y, x), tensor: 16 (over z, core).
Axes of the slice: x: 4, y: 4, z: 8, core: 2. Of those that a mesh axis runs over, the one named last changes fastest.
Arguments:
- tokens: bfloat16 [4096, 4096], P('dp'), may hold values from -6 to 6
- cotangent: bfloat16 [4096, 4096], P('dp'), may hold values from -6 to 6
- gate_weight: bfloat16 [4096, 14336], P('dp', 'tensor'), may hold values from -0.09375 to 0.09375
- up_weight: bfloat16 [4096, 14336], P('dp', 'tensor'), may hold values from -0.09375 to 0.09375
- down_weight: bfloat16 [14336, 4096], P('tensor', 'dp'), may hold values from -0.046875 to 0.046875
Outputs:
- input_grad: bfloat16 [4096, 4096], P('dp')
- gate_weight_grad: bfloat16 [4096, 14336], P('dp', 'tensor')
- up_weight_grad: bfloat16 [4096, 14336], P('dp', 'tensor')
- down_weight_grad: bfloat16 [14336, 4096], P('tensor', 'dp')
The draws below stay inside these ranges and needn't reach their ends.
All inputs are finite; a program needn't handle non-finite values.
Results may differ from the reference program's by a relative error of at most 0.027.
Values may be sent and summed in bfloat16 or wider, within the bound.
No kernel may reach another device: no remote copies, remote signals or barrier semaphores. Data moves between devices by JAX's collectives and lax.ppermute only.
A program may use at most 192 MiB of HBM per device.

```python
import jax
import jax.numpy as jnp
from jax import lax

D = 4096
FF = 14336
TOK_DEV = 256
TOKENS = 4096
N_DP = 16
N_TENSOR = 16


def strengthened(result, own_key, source, target, parts, factor):
    owner, partner = [(jnp.arange(result.shape[dim]) // (result.shape[dim] // parts)).reshape([-1 if axis == dim else 1 for axis in range(result.ndim)]) for dim in (source, target)]
    chosen = jax.random.permutation(own_key, parts)[partner]
    strong = (owner == chosen) | (owner == (partner + parts // 2) % parts)
    return jnp.where(strong, factor * result, result)


def block_levels(key, shape, cuts, smallest, top_value):
    gain, own = 1.0, jax.random.fold_in(key, 6)
    for dim, parts in cuts:
        steps = jnp.exp(jax.random.uniform(jax.random.fold_in(own, dim), (parts,), jnp.float32, smallest / len(cuts), top_value / len(cuts)))
        gain = gain * jnp.repeat(steps, shape[dim] // parts).reshape([-1 if axis == dim else 1 for axis in range(len(shape))])
    return gain


def gaussian(key, shape, scale, most, cuts=(), kind=jnp.bfloat16):
    array = jax.random.normal(key, shape, jnp.float32) * scale
    if len(cuts) > 0:
        array = block_levels(key, shape, cuts, -0.22, 0.18) * array
    return jnp.clip(array, min=-most, max=most).astype(kind)


def noise_with(rng, extent, spread, bound, split, heavy, dtype=jnp.bfloat16):
    drawn = spread * jax.random.normal(rng, extent, jnp.float32)
    if split:
        drawn = drawn * block_levels(rng, extent, split, -0.22, 0.18)
    return jnp.clip(strengthened(drawn, jax.random.fold_in(rng, 3), *heavy), -bound, bound).astype(dtype)


def setup_inputs(seed: int = 0) -> dict:
    arg_keys = jax.random.split(jax.random.key(seed), 6)
    return {
        "tokens": noise_with(arg_keys[0], (TOKENS, D), 1.0, 6.0, ((0, 16),), (0, 1, 16, 2.0)),
        "cotangent": noise_with(arg_keys[1], (TOKENS, D), 1.0, 6.0, ((0, 16),), (0, 1, 16, 2.0)),
        "gate_weight": gaussian(arg_keys[2], (D, FF), D ** -0.5, 0.09375, ((0, 16), (1, 16))),
        "up_weight": gaussian(arg_keys[3], (D, FF), D ** -0.5, 0.09375, ((0, 16), (1, 16))),
        "down_weight": gaussian(arg_keys[4], (FF, D), FF ** -0.5, 0.046875, ((0, 16), (1, 16))),
    }


def reference(tokens, cotangent, gate_weight, up_weight, down_weight):
    f32 = jnp.float32
    bf16 = jnp.bfloat16
    gate = jnp.dot(tokens, gate_weight, preferred_element_type=f32)
    up = jnp.dot(tokens, up_weight, preferred_element_type=f32)
    hidden_grad = jnp.dot(cotangent, down_weight.T, preferred_element_type=f32)
    sigmoid_gate = jax.nn.sigmoid(gate)
    activated = gate * sigmoid_gate
    hidden = (activated * up).astype(bf16)
    gate_grad = (hidden_grad * up * sigmoid_gate * (1.0 + gate * (1.0 - sigmoid_gate))).astype(bf16)
    up_grad = (hidden_grad * activated).astype(bf16)

    share = FF // N_TENSOR
    grad_groups = gate_grad.reshape(TOKENS, N_TENSOR, share).transpose(1, 0, 2)
    upgrad_groups = up_grad.reshape(TOKENS, N_TENSOR, share).transpose(1, 0, 2)
    gate_groups = gate_weight.reshape(D, N_TENSOR, share).transpose(1, 0, 2)
    up_groups = up_weight.reshape(D, N_TENSOR, share).transpose(1, 0, 2)

    def add_share(running, items):
        grad_a, grad_b, weight_a, weight_b = items
        term = jnp.dot(grad_a, weight_a.T, preferred_element_type=f32) + jnp.dot(grad_b, weight_b.T, preferred_element_type=f32)
        rounded = lax.optimization_barrier(term.astype(bf16))
        return running + rounded.astype(f32), None

    summed, _ = lax.scan(add_share, jnp.zeros((TOKENS, D), f32), (grad_groups, upgrad_groups, gate_groups, up_groups))
    input_grad = summed.astype(bf16)

    token_groups = tokens.reshape(N_DP, TOK_DEV, D)
    cot_groups = cotangent.reshape(N_DP, TOK_DEV, D)
    gg_groups = gate_grad.reshape(N_DP, TOK_DEV, FF)
    ug_groups = up_grad.reshape(N_DP, TOK_DEV, FF)
    hidden_groups = hidden.reshape(N_DP, TOK_DEV, FF)

    def rounded_term(left, right):
        term = jnp.dot(left.T, right, preferred_element_type=f32)
        return lax.optimization_barrier(term.astype(bf16)).astype(f32)

    def add_group(running, items):
        inputs, cots, ggrad, ugrad, hid = items
        return (running[0] + rounded_term(inputs, ggrad),
                running[1] + rounded_term(inputs, ugrad),
                running[2] + rounded_term(hid, cots)), None

    start_sums = (jnp.zeros((D, FF), f32), jnp.zeros((D, FF), f32), jnp.zeros((FF, D), f32))
    sums, _ = lax.scan(add_group, start_sums, (token_groups, cot_groups, gg_groups, ug_groups, hidden_groups))
    return input_grad, sums[0].astype(bf16), sums[1].astype(bf16), sums[2].astype(bf16)
```

```python
import functools

import jax
import jax.numpy as jnp
from jax import lax
from jax.experimental import pallas as pl
from jax.experimental.pallas import tpu as pltpu
from jax.sharding import Mesh, PartitionSpec as P

BF = jnp.bfloat16
F32 = jnp.float32
NY, NX, NZ, NC = 4, 4, 8, 2
TOK = 256
D = 4096
SHARE = 896
Q = SHARE // NX
DB = 256
ROWS = 3 * Q
HALF = D // 2
PARAMS = pltpu.CompilerParams(vmem_limit_bytes=56 * 1024 * 1024)
ANY = pl.BlockSpec(memory_space=pl.ANY)
VM = pl.BlockSpec(memory_space=pltpu.VMEM)
SM = pl.BlockSpec(memory_space=pltpu.SMEM)


def shift(value, axis, size, step):
    return lax.ppermute(value, axis, [(i, (i + step) % size) for i in range(size)])


def flip(value):
    return value.astype(F32).T.astype(BF)


def cut_kernel(pos, g_ref, u_ref, d_ref, o_ref, gt, ut):
    gt[...] = flip(g_ref[...])
    ut[...] = flip(u_ref[...])
    x = pos[1]
    for r in range(NX):
        q0 = pl.multiple_of(lax.rem(x + r, NX) * Q, 16)
        o_ref[r, 0:Q, :] = gt[pl.ds(q0, Q), :]
        o_ref[r, Q : 2 * Q, :] = ut[pl.ds(q0, Q), :]
        o_ref[r, 2 * Q : ROWS, :] = d_ref[pl.ds(q0, Q), :]


def cut(pos, g, u, d):
    return pl.pallas_call(
        cut_kernel,
        out_shape=jax.ShapeDtypeStruct((NX, ROWS, DB), BF),
        in_specs=[SM, VM, VM, VM],
        out_specs=VM,
        scratch_shapes=[pltpu.VMEM((SHARE, DB), BF), pltpu.VMEM((SHARE, DB), BF)],
        compiler_params=PARAMS,
        name="cut",
    )(pos, g, u, d)


def main_kernel(pos, *refs):
    slabs = refs[:4]
    tok_own, cot_own, rest = refs[4:7]
    gt_ref, gg_ref, w_ref = refs[7:10]
    tv, cv, wsem, tsem, csem = refs[10:]
    y, x = pos[0], pos[1]
    wcopies = []
    for ry in range(NY):
        for rx in range(NX):
            off = pl.multiple_of((lax.rem(y + ry, NY) * NX + lax.rem(x + rx, NX)) * DB, DB)
            wcopies.append(
                pltpu.make_async_copy(
                    slabs[ry].at[rx], w_ref.at[:, pl.ds(off, DB)], wsem.at[ry * NX + rx]
                )
            )
    tcopies = [
        pltpu.make_async_copy(tok_own if j == 0 else rest.at[j - 1], tv.at[j], tsem.at[j])
        for j in range(NX)
    ]
    ccopies = [
        pltpu.make_async_copy(cot_own if j == 0 else rest.at[NX - 1 + j - 1], cv.at[j], csem.at[j])
        for j in range(NX)
    ]
    for copy in wcopies:
        copy.start()
    for j in range(NX):
        tcopies[j].start()
        ccopies[j].start()
    for copy in wcopies:
        copy.wait()
    nt = (((1,), (1,)), ((), ()))
    for j in range(NX):
        tcopies[j].wait()
        gate_up = lax.dot_general(w_ref[0 : 2 * Q, :], tv[j], nt, preferred_element_type=F32)
        ccopies[j].wait()
        hidden_grad = lax.dot_general(w_ref[2 * Q : ROWS, :], cv[j], nt, preferred_element_type=F32)
        gate, up = gate_up[0:Q], gate_up[Q : 2 * Q]
        s = jax.nn.sigmoid(gate)
        act = gate * s
        rows = slice(j * TOK, (j + 1) * TOK)
        gate_grad = hidden_grad * up * s * (1.0 + gate * (1.0 - s))
        up_grad = hidden_grad * act
        gt_ref[0:Q, rows] = gate_grad.astype(BF)
        gt_ref[Q : 2 * Q, rows] = up_grad.astype(BF)
        gt_ref[2 * Q : ROWS, rows] = (act * up).astype(BF)
        gg_ref[rows, :] = flip(gt_ref[0 : 2 * Q, rows])


def forward(pos, slabs, tok, cot, rest):
    return pl.pallas_call(
        main_kernel,
        out_shape=(
            jax.ShapeDtypeStruct((ROWS, NX * TOK), BF),
            jax.ShapeDtypeStruct((NX * TOK, 2 * Q), BF),
            jax.ShapeDtypeStruct((ROWS, D), BF),
        ),
        in_specs=[SM] + [ANY] * 7,
        out_specs=(VM, VM, VM),
        scratch_shapes=[
            pltpu.VMEM((NX, TOK, D), BF),
            pltpu.VMEM((NX, TOK, D), BF),
            pltpu.SemaphoreType.DMA((NX * NY,)),
            pltpu.SemaphoreType.DMA((NX,)),
            pltpu.SemaphoreType.DMA((NX,)),
        ],
        compiler_params=PARAMS,
        name="forward",
    )(pos, *slabs, tok, cot, rest)


def wgrad_kernel(ry, pos, gt_ref, tok_own, cot_own, rest, o_ref, tv, cv, tsem, csem):
    y, x = pos[0], pos[1]
    cols = pl.ds(pl.multiple_of(lax.rem(y + ry, NY) * (NX * DB), NX * DB), NX * DB)
    copies = []
    for j in range(NX):
        t_src = tok_own if j == 0 else rest.at[j - 1]
        c_src = cot_own if j == 0 else rest.at[NX - 1 + j - 1]
        rows = pl.ds(j * TOK, TOK)
        copies.append(pltpu.make_async_copy(t_src.at[:, cols], tv.at[rows, :], tsem.at[j]))
        copies.append(pltpu.make_async_copy(c_src.at[:, cols], cv.at[rows, :], csem.at[j]))
    for copy in copies:
        copy.start()
    for copy in copies:
        copy.wait()
    for rx in range(NX):
        part = pl.ds(pl.multiple_of(lax.rem(x + rx, NX) * DB, DB), DB)
        o_ref[rx, 0 : 2 * Q, :] = jnp.dot(
            gt_ref[0 : 2 * Q, :], tv[:, part], preferred_element_type=F32
        ).astype(BF)
        o_ref[rx, 2 * Q : ROWS, :] = jnp.dot(
            gt_ref[2 * Q : ROWS, :], cv[:, part], preferred_element_type=F32
        ).astype(BF)


def wgrad(ry, pos, gt, tok, cot, rest):
    return pl.pallas_call(
        functools.partial(wgrad_kernel, ry),
        out_shape=jax.ShapeDtypeStruct((NX, ROWS, DB), BF),
        in_specs=[SM, VM, ANY, ANY, ANY],
        out_specs=VM,
        scratch_shapes=[
            pltpu.VMEM((NX * TOK, NX * DB), BF),
            pltpu.VMEM((NX * TOK, NX * DB), BF),
            pltpu.SemaphoreType.DMA((NX,)),
            pltpu.SemaphoreType.DMA((NX,)),
        ],
        compiler_params=PARAMS,
        name="wgrad",
    )(pos, gt, tok, cot, rest)


def igrad_kernel(flipped, pos, gg_ref, w_ref, o_ref, wv, sem):
    c = pos[3]
    half = 1 - c if flipped else c
    copy = pltpu.make_async_copy(
        w_ref.at[pl.ds(0, 2 * Q), pl.ds(pl.multiple_of(half * HALF, HALF), HALF)], wv, sem
    )
    @pl.when(pl.program_id(0) == 0)
    def _():
        copy.start()
        copy.wait()
    o_ref[...] = jnp.dot(gg_ref[...], wv[...], preferred_element_type=F32).astype(BF)


def igrad(flipped, pos, gg, w):
    return pl.pallas_call(
        functools.partial(igrad_kernel, flipped),
        grid=(NX,),
        out_shape=jax.ShapeDtypeStruct((NX * TOK, HALF), BF),
        in_specs=[SM, pl.BlockSpec((TOK, 2 * Q), lambda j: (j, 0)), ANY],
        out_specs=pl.BlockSpec((TOK, HALF), lambda j: (j, 0)),
        scratch_shapes=[pltpu.VMEM((2 * Q, HALF), BF), pltpu.SemaphoreType.DMA],
        compiler_params=PARAMS,
        name="igrad",
    )(pos, gg, w)


def add(*parts):
    total = parts[0].astype(F32)
    for part in parts[1:]:
        total = total + part.astype(F32)
    return total.astype(BF)


def reduce_four(parts, axis):
    far = parts[2]
    mid = far.shape[0] // 2
    up = shift(far[:mid], axis, 4, 1)
    down = shift(far[mid:], axis, 4, -1)
    to_next = jnp.concatenate([add(parts[1][:mid], up), parts[1][mid:]], axis=0)
    to_prev = jnp.concatenate([parts[3][:mid], add(parts[3][mid:], down)], axis=0)
    return add(parts[0], shift(to_next, axis, 4, 1), shift(to_prev, axis, 4, -1))


def reduce_eight(value, z):
    parts = value.reshape(NZ, TOK // NZ, value.shape[1])
    part = lambda k: lax.dynamic_index_in_dim(parts, lax.rem(z + k + NZ, NZ), 0, keepdims=False)
    mid = TOK // NZ // 2
    far = part(4)
    right = shift(far[:mid], "z", NZ, 1)
    left = shift(far[mid:], "z", NZ, -1)
    for k in (3, 2, 1):
        mine_r, mine_l = part(k), part(-k)
        if k == 3:
            right = jnp.concatenate([add(mine_r[:mid], right), mine_r[mid:]], axis=0)
            left = jnp.concatenate([mine_l[:mid], add(mine_l[mid:], left)], axis=0)
        else:
            right, left = add(mine_r, right), add(mine_l, left)
        right = shift(right, "z", NZ, 1)
        left = shift(left, "z", NZ, -1)
    own = add(part(0), right, left)
    slots = {0: own}
    right = left = own
    for k in (1, 2, 3):
        right, left = shift(right, "z", NZ, 1), shift(left, "z", NZ, -1)
        slots[NZ - k], slots[k] = right, left
    slots[4] = jnp.concatenate(
        [shift(right[:mid], "z", NZ, 1), shift(left[mid:], "z", NZ, -1)], axis=0
    )
    return jnp.stack([slots[k] for k in range(NZ)])


def place_kernel(pos, a_ref, b_ref, o_ref):
    z, c = pos[2], pos[3]
    rows = TOK // NZ
    for k in range(NZ):
        at = pl.ds(pl.multiple_of(lax.rem(z + k, NZ) * rows, rows), rows)
        o_ref[at, pl.ds(pl.multiple_of(c * HALF, HALF), HALF)] = a_ref[k]
        o_ref[at, pl.ds(pl.multiple_of((1 - c) * HALF, HALF), HALF)] = b_ref[k]


def place(pos, mine, other):
    return pl.pallas_call(
        place_kernel,
        out_shape=jax.ShapeDtypeStruct((TOK, D), BF),
        in_specs=[SM, VM, VM],
        out_specs=VM,
        compiler_params=PARAMS,
        name="place",
    )(pos, mine, other)


def join_kernel(pos, a_ref, b_ref, c_ref, d_ref, g_ref, u_ref, o_ref, gt, ut):
    x = pos[1]
    for r, ref in enumerate((a_ref, b_ref, c_ref, d_ref)):
        at = pl.ds(pl.multiple_of(lax.rem(x + r, NX) * Q, 16), Q)
        gt[at, :] = ref[0:Q, :]
        ut[at, :] = ref[Q : 2 * Q, :]
        o_ref[at, :] = ref[2 * Q : ROWS, :]
    g_ref[...] = flip(gt[...])
    u_ref[...] = flip(ut[...])


def join(pos, parts):
    return pl.pallas_call(
        join_kernel,
        out_shape=(
            jax.ShapeDtypeStruct((DB, SHARE), BF),
            jax.ShapeDtypeStruct((DB, SHARE), BF),
            jax.ShapeDtypeStruct((SHARE, DB), BF),
        ),
        in_specs=[SM] + [VM] * 4,
        out_specs=(VM, VM, VM),
        scratch_shapes=[pltpu.VMEM((SHARE, DB), BF), pltpu.VMEM((SHARE, DB), BF)],
        compiler_params=PARAMS,
        name="join",
    )(pos, *parts)


def per_device(tokens, cotangent, gate_weight, up_weight, down_weight):
    y, x, z, c = (lax.axis_index(a).astype(jnp.int32) for a in ("y", "x", "z", "c"))
    pos = jnp.stack([y, x, z, c])
    with jax.named_scope("tokens"):
        step = TOK // (NZ * NC)
        start = (z * NC + c) * step
        seed = jnp.stack(
            [lax.dynamic_slice_in_dim(a, start, step, 0) for a in (tokens, cotangent)]
        )
        seeds = [shift(seed, "x", NX, -r) for r in (1, 2, 3)]
        seeds = jnp.concatenate([s[:1] for s in seeds] + [s[1:] for s in seeds], axis=0)
        rest = lax.all_gather(seeds, ("z", "c"), axis=1, tiled=True)
    with jax.named_scope("weights"):
        cuts = cut(pos, gate_weight, up_weight, down_weight)
        mine = [cuts[0]] + [shift(cuts[NX - r], "x", NX, -r) for r in (1, 2, 3)]
        slab = jnp.stack(mine)
        above, below = shift(slab, "y", NY, -1), shift(slab, "y", NY, 1)
        across = jnp.concatenate(
            [shift(above[:2], "y", NY, -1), shift(below[2:], "y", NY, 1)], axis=0
        )
        slabs = [slab, above, across, below]
    with jax.named_scope("forward"):
        gt, gg, w = forward(pos, slabs, tokens, cotangent, rest)
    with jax.named_scope("grads"):
        other = igrad(True, pos, gg, w)
        w2 = wgrad(2, pos, gt, tokens, cotangent, rest)
        mine = igrad(False, pos, gg, w)
        w1, w3, w0 = (wgrad(r, pos, gt, tokens, cotangent, rest) for r in (1, 3, 0))
    with jax.named_scope("input"):
        chip = add(mine, shift(other, "c", NC, 1)).reshape(NX, TOK, HALF)
        row = reduce_four([chip[r] for r in range(NX)], "x")
        col = reduce_eight(row, z)
        input_grad = place(pos, col, shift(col, "c", NC, 1))
    with jax.named_scope("weight"):
        summed = reduce_four([w0, w1, w2, w3], "y")
        parts = [summed[0]] + [shift(summed[NX - r], "x", NX, -r) for r in (1, 2, 3)]
        gate_grad, up_grad, down_grad = join(pos, parts)
    return input_grad, gate_grad, up_grad, down_grad


def solution(mesh):
    grid = Mesh(mesh.devices.reshape(NY, NX, NZ, NC), ("y", "x", "z", "c"))
    dp, tensor = ("y", "x"), ("z", "c")
    return jax.shard_map(
        per_device,
        mesh=grid,
        in_specs=(P(dp, None), P(dp, None), P(dp, tensor), P(dp, tensor), P(tensor, dp)),
        out_specs=(P(dp, None), P(dp, tensor), P(dp, tensor), P(tensor, dp)),
        check_vma=False,
    )
```

```python
import functools

import jax
import jax.numpy as jnp
from jax import lax
from jax.experimental import pallas as pl
from jax.experimental.pallas import tpu as pltpu
from jax.sharding import Mesh, PartitionSpec as P

BF = jnp.bfloat16
F32 = jnp.float32
NY, NX, NZ, NC = 4, 4, 8, 2
TOK = 256
D = 4096
SHARE = 896
Q = SHARE // NX
DB = 256
ROWS = 3 * Q
HALF = D // 2
PARAMS = pltpu.CompilerParams(vmem_limit_bytes=56 * 1024 * 1024)
ANY = pl.BlockSpec(memory_space=pl.ANY)
VM = pl.BlockSpec(memory_space=pltpu.VMEM)
SM = pl.BlockSpec(memory_space=pltpu.SMEM)


def shift(value, axis, size, step):
    return lax.ppermute(value, axis, [(i, (i + step) % size) for i in range(size)])


def flip(value):
    return value.astype(BF).T


ORDER = (0, 1, 3, 2)
CHUNKS = (0, 1, 2, 3, 5, 6, 7, 4)
STEP = TOK // NZ
CHUNK = NX * STEP


def cut_kernel(pos, g_ref, u_ref, d_ref, o0, o1, o2, o3, gt, ut):
    gt[...] = flip(g_ref[...])
    ut[...] = flip(u_ref[...])
    x = pos[1]
    for r, o_ref in enumerate((o0, o1, o2, o3)):
        q0 = pl.multiple_of(lax.rem(x + r, NX) * Q, 16)
        o_ref[0:Q, :] = gt[pl.ds(q0, Q), :]
        o_ref[Q : 2 * Q, :] = ut[pl.ds(q0, Q), :]
        o_ref[2 * Q : ROWS, :] = d_ref[pl.ds(q0, Q), :]


def cut(pos, g, u, d):
    return pl.pallas_call(
        cut_kernel,
        out_shape=(jax.ShapeDtypeStruct((ROWS, DB), BF),) * NX,
        in_specs=[SM, VM, VM, VM],
        out_specs=(VM,) * NX,
        scratch_shapes=[pltpu.VMEM((SHARE, DB), BF), pltpu.VMEM((SHARE, DB), BF)],
        compiler_params=PARAMS,
        name="cut",
    )(pos, g, u, d)


def forward_kernel(places, pos, *refs):
    n = len(places)
    pieces = refs[:n]
    tok, cot, rest, near, far = refs[n : n + 5]
    gt_ref, outs = refs[n + 5], refs[n + 6 : n + 10]
    wv, tv, cv, gg_ref, gz_ref, *held, wsem, tsem, csem, osem = refs[n + 10 :]
    y, x, z, c = pos[0], pos[1], pos[2], pos[3]
    copies = []
    for ref, (ry, rx, count) in zip(pieces, places):
        for k in range(count):
            at = (lax.rem(y + ry, NY) * NX + lax.rem(x + rx + k, NX)) * DB
            copies.append(
                pltpu.make_async_copy(
                    ref if count == 1 else ref.at[k],
                    wv.at[:, pl.ds(pl.multiple_of(at, DB), DB)],
                    wsem.at[ry * NX + rx + k],
                )
            )
    tcopies, ccopies = [], []
    for slot, r in enumerate(ORDER):
        rows = pl.ds(slot * TOK, TOK)
        tcopies.append(
            pltpu.make_async_copy(tok if r == 0 else rest.at[r - 1], tv.at[rows], tsem.at[slot])
        )
        if r in (0, 2):
            src = cot if r == 0 else rest.at[3]
            ccopies.append([pltpu.make_async_copy(src, cv.at[rows], csem.at[slot, 0])])
        else:
            ccopies.append(
                [
                    pltpu.make_async_copy(
                        src.at[(r - 1) // 2],
                        cv.at[rows, pl.ds(pl.multiple_of(col * HALF, HALF), HALF)],
                        csem.at[slot, k],
                    )
                    for k, (src, col) in enumerate(((near, c), (far, 1 - c)))
                ]
            )
    for copy in copies:
        copy.start()
    for slot in range(NX):
        tcopies[slot].start()
        for copy in ccopies[slot]:
            copy.start()
    for copy in copies:
        copy.wait()
    nt = (((1,), (1,)), ((), ()))
    for slot in range(NX):
        rows = slice(slot * TOK, (slot + 1) * TOK)
        tcopies[slot].wait()
        gate = lax.dot_general(tv[rows], wv[0:Q, :], nt, preferred_element_type=F32)
        up = lax.dot_general(tv[rows], wv[Q : 2 * Q, :], nt, preferred_element_type=F32)
        for copy in ccopies[slot]:
            copy.wait()
        hidden_grad = lax.dot_general(
            cv[rows], wv[2 * Q : ROWS, :], nt, preferred_element_type=F32
        )
        s = jax.nn.sigmoid(gate)
        act = gate * s
        gate_grad = (hidden_grad * up * s * (1.0 + gate * (1.0 - s))).astype(BF)
        up_grad = (hidden_grad * act).astype(BF)
        gg_ref[rows, 0:Q] = gate_grad
        gg_ref[rows, Q : 2 * Q] = up_grad
        gt_ref[0:Q, rows] = gate_grad.T
        gt_ref[Q : 2 * Q, rows] = up_grad.T
        gt_ref[2 * Q : ROWS, rows] = flip(act * up)
    for i, k in enumerate(CHUNKS):
        for slot in range(NX):
            at = pl.multiple_of(slot * TOK + lax.rem(z + k, NZ) * STEP, STEP)
            gz_ref[(i * NX + slot) * STEP : (i * NX + slot + 1) * STEP, :] = gg_ref[
                pl.ds(at, STEP), :
            ]
    writes = []
    for k, half in enumerate((1 - c, c)):
        far_ref, rest_ref = held[2 * k : 2 * k + 2]
        for i in range(HALF // 512):
            cols = pl.ds(pl.multiple_of(half * HALF + i * 512, 512), 512)
            part = jnp.dot(gz_ref[...], wv[0 : 2 * Q, cols], preferred_element_type=F32).astype(BF)
            rest_ref[:, i * 512 : (i + 1) * 512] = part[0 : 7 * CHUNK]
            far_ref[:, i * 512 : (i + 1) * 512] = part[7 * CHUNK :]
        for m, ref in enumerate((far_ref, rest_ref)):
            writes.append(pltpu.make_async_copy(ref, outs[2 * k + m], osem.at[2 * k + m]))
            writes[-1].start()
    for copy in writes:
        copy.wait()


def forward(pos, places, pieces, tok, cot, rest, near, far):
    parts = tuple(jax.ShapeDtypeStruct((k * CHUNK, HALF), BF) for k in (1, 7))
    return pl.pallas_call(
        functools.partial(forward_kernel, places),
        out_shape=(
            jax.ShapeDtypeStruct((ROWS, NX * TOK), BF),
        )
        + parts * 2,
        in_specs=[SM] + [ANY] * (len(pieces) + 5),
        out_specs=(VM,) + (ANY,) * 4,
        scratch_shapes=[
            pltpu.VMEM((ROWS, D), BF),
            pltpu.VMEM((NX * TOK, D), BF),
            pltpu.VMEM((NX * TOK, D), BF),
            pltpu.VMEM((NX * TOK, 2 * Q), BF),
            pltpu.VMEM((NX * TOK, 2 * Q), BF),
            *[pltpu.VMEM(part.shape, BF) for part in parts * 2],
            pltpu.SemaphoreType.DMA((NX * NY,)),
            pltpu.SemaphoreType.DMA((NX,)),
            pltpu.SemaphoreType.DMA((NX, 2)),
            pltpu.SemaphoreType.DMA((4,)),
        ],
        compiler_params=PARAMS,
        name="forward",
    )(pos, *pieces, tok, cot, rest, near, far)


def wgrad_kernel(ry, pos, gt_ref, tok, cot, rest, near, far, *refs):
    *outs, tv, cv, tsem, csem = refs[-6 if ry == 2 else -5 :]
    out = lambda rx: outs[rx // 2].at[rx % 2] if ry == 2 else outs[0].at[rx]
    y, x, c = pos[0], pos[1], pos[3]
    slab = lax.rem(y + ry, NY)
    cols = pl.ds(pl.multiple_of(slab * (NX * DB), NX * DB), NX * DB)
    inner = pl.ds(pl.multiple_of(lax.rem(slab, 2) * (NX * DB), NX * DB), NX * DB)
    here = slab // 2 == c
    tcopies, ccopies = [], []
    for slot, r in enumerate(ORDER):
        rows = pl.ds(slot * TOK, TOK)
        src = tok if r == 0 else rest.at[r - 1]
        tcopies.append(
            pltpu.make_async_copy(src.at[:, cols], tv.at[rows, :], tsem.at[slot])
        )
        if r in (0, 2):
            src = cot if r == 0 else rest.at[3]
            ccopies.append((None, pltpu.make_async_copy(src.at[:, cols], cv.at[rows, :], csem.at[slot])))
        else:
            for k, src in enumerate((near, far)):
                ccopies.append(
                    (
                        k,
                        pltpu.make_async_copy(
                            src.at[(r - 1) // 2, :, inner], cv.at[rows, :], csem.at[slot]
                        ),
                    )
                )
    for copy in tcopies:
        copy.start()

    def each(act):
        for k, copy in ccopies:
            if k is None:
                act(copy)
            else:
                pl.when(here if k == 0 else jnp.logical_not(here))(functools.partial(act, copy))

    each(lambda copy: copy.start())
    for copy in tcopies:
        copy.wait()
    for rx in range(NX):
        part = pl.ds(pl.multiple_of(lax.rem(x + rx, NX) * DB, DB), DB)
        out(rx)[0 : 2 * Q, :] = jnp.dot(
            gt_ref[0 : 2 * Q, :], tv[:, part], preferred_element_type=F32
        ).astype(BF)
    each(lambda copy: copy.wait())
    for rx in range(NX):
        part = pl.ds(pl.multiple_of(lax.rem(x + rx, NX) * DB, DB), DB)
        out(rx)[2 * Q : ROWS, :] = jnp.dot(
            gt_ref[2 * Q : ROWS, :], cv[:, part], preferred_element_type=F32
        ).astype(BF)


def wgrad(ry, pos, gt, tok, cot, rest, near, far, *after):
    shape = jax.ShapeDtypeStruct((NX // 2 if ry == 2 else NX, ROWS, DB), BF)
    return pl.pallas_call(
        functools.partial(wgrad_kernel, ry),
        out_shape=(shape, shape) if ry == 2 else shape,
        in_specs=[SM, VM] + [ANY] * (5 + len(after)),
        out_specs=(VM, VM) if ry == 2 else VM,
        scratch_shapes=[
            pltpu.VMEM((NX * TOK, NX * DB), BF),
            pltpu.VMEM((NX * TOK, NX * DB), BF),
            pltpu.SemaphoreType.DMA((NX,)),
            pltpu.SemaphoreType.DMA((NX,)),
        ],
        compiler_params=PARAMS,
        name="wgrad",
    )(pos, gt, tok, cot, rest, near, far, *after)


def add(*parts):
    total = parts[0].astype(F32)
    for part in parts[1:]:
        total = total + part.astype(F32)
    return total.astype(BF)


def far_step(far, axis):
    mid = far.shape[0] // 2
    return shift(far[:mid], axis, 4, 1), shift(far[mid:], axis, 4, -1)


def near_step(after, before, up, down, axis):
    mid = up.shape[0]
    to_next = jnp.concatenate([add(after[:mid], up), after[mid:]], axis=0)
    to_prev = jnp.concatenate([before[:mid], add(before[mid:], down)], axis=0)
    return shift(to_next, axis, 4, 1), shift(to_prev, axis, 4, -1), (to_next, to_prev)


def tie(values, *others):
    return lax.optimization_barrier((values, others))[0]


def gather_eight(own, flying):
    mid = TOK // NZ // 2
    slots = {0: own}
    right = left = own
    for k in (1, 2, 3):
        right, left = shift(right, "z", NZ, 1), shift(left, "z", NZ, -1)
        slots[NZ - k], slots[k] = right, left
    right, left, flying = tie((right, left, flying))
    slots[4] = jnp.concatenate(
        [shift(right[:mid], "z", NZ, 1), shift(left[mid:], "z", NZ, -1)], axis=0
    )
    return jnp.stack([slots[k] for k in range(NZ)]), flying


def place_kernel(pos, a_ref, b_ref, o_ref):
    z, c = pos[2], pos[3]
    rows = TOK // NZ
    for k in range(NZ):
        at = pl.ds(pl.multiple_of(lax.rem(z + k, NZ) * rows, rows), rows)
        o_ref[at, pl.ds(pl.multiple_of(c * HALF, HALF), HALF)] = a_ref[k]
        o_ref[at, pl.ds(pl.multiple_of((1 - c) * HALF, HALF), HALF)] = b_ref[k]


def place(pos, mine, other):
    return pl.pallas_call(
        place_kernel,
        out_shape=jax.ShapeDtypeStruct((TOK, D), BF),
        in_specs=[SM, VM, VM],
        out_specs=VM,
        compiler_params=PARAMS,
        name="place",
    )(pos, mine, other)


def join_kernel(pos, a_ref, b_ref, c_ref, d_ref, g_ref, u_ref, o_ref, gt, ut):
    x = pos[1]
    for r, ref in enumerate((a_ref, b_ref, c_ref, d_ref)):
        at = pl.ds(pl.multiple_of(lax.rem(x + r, NX) * Q, 16), Q)
        gt[at, :] = ref[0:Q, :]
        ut[at, :] = ref[Q : 2 * Q, :]
        o_ref[at, :] = ref[2 * Q : ROWS, :]
    g_ref[...] = flip(gt[...])
    u_ref[...] = flip(ut[...])


def join(pos, parts):
    return pl.pallas_call(
        join_kernel,
        out_shape=(
            jax.ShapeDtypeStruct((DB, SHARE), BF),
            jax.ShapeDtypeStruct((DB, SHARE), BF),
            jax.ShapeDtypeStruct((SHARE, DB), BF),
        ),
        in_specs=[SM] + [VM] * 4,
        out_specs=(VM, VM, VM),
        scratch_shapes=[pltpu.VMEM((SHARE, DB), BF), pltpu.VMEM((SHARE, DB), BF)],
        compiler_params=PARAMS,
        name="join",
    )(pos, *parts)


def per_device(tokens, cotangent, gate_weight, up_weight, down_weight):
    y, x, z, c = (lax.axis_index(a).astype(jnp.int32) for a in ("y", "x", "z", "c"))
    pos = jnp.stack([y, x, z, c])
    with jax.named_scope("tokens"):
        step = TOK // (NZ * NC)
        start = (z * NC + c) * step
        seed_t, seed_c = (
            lax.dynamic_slice_in_dim(a, start, step, 0)[None] for a in (tokens, cotangent)
        )
        two = shift(jnp.concatenate([seed_t, seed_c]), "x", NX, 2)
        seeds = [shift(seed_t, "x", NX, -1), two[:1], shift(seed_t, "x", NX, 1), two[1:]]
        cuts = cut(pos, gate_weight, up_weight, down_weight)
        seeds = tie(jnp.concatenate(seeds), cuts)
        rest = lax.all_gather(seeds, ("z", "c"), axis=1, tiled=True)
    with jax.named_scope("weights"):
        cuts = tie(cuts, seeds)
        mine = [shift(cuts[NX - r], "x", NX, -r) for r in (1, 2, 3)]
        above0, below0 = shift(cuts[0], "y", NY, -1), shift(cuts[0], "y", NY, 1)
    half = lax.dynamic_slice_in_dim(cotangent, c * HALF, HALF, 1)
    mine, above0, below0, half = tie((mine, above0, below0, half))
    with jax.named_scope("weights"):
        slab = jnp.stack(mine)
        above, below = shift(slab, "y", NY, -1), shift(slab, "y", NY, 1)
    with jax.named_scope("tokens"):
        from_next, from_prev = shift(half, "x", NX, -1), shift(half, "x", NX, 1)
    above, below, from_next, from_prev = tie((above, below, from_next, from_prev))
    with jax.named_scope("weights"):
        across01 = shift(jnp.stack([above0, above[0]]), "y", NY, -1)
        across23 = shift(below[1:], "y", NY, 1)
        pieces = [cuts[0], *mine, above0, above, below0, below, across01, across23]
        places = [(0, 0, 1), (0, 1, 1), (0, 2, 1), (0, 3, 1)]
        places += [(1, 0, 1), (1, 1, 3), (3, 0, 1), (3, 1, 3), (2, 0, 2), (2, 2, 2)]
    with jax.named_scope("tokens"):
        near = jnp.stack([from_next, from_prev])
        far = shift(near, "c", NC, 1)
    acts = (tokens, cotangent, rest, near, far)
    with jax.named_scope("forward"):
        gt, far_o, rest_o, far_m, rest_m = forward(pos, places, pieces, *acts)
    ring = lambda a, b: (shift(a, "z", NZ, 1), shift(b, "z", NZ, -1))
    with jax.named_scope("grads"):
        far_in, rest_in = shift(far_o, "c", NC, 1), shift(rest_o, "c", NC, 1)
        far, mid = add(far_m, far_in), CHUNK // 2
        right, left = ring(far[:mid], far[mid:])
        w2 = wgrad(2, pos, gt, *acts, far)
        up_y, down_y = shift(w2[0], "y", NY, 1), shift(w2[1], "y", NY, -1)
        right, left, rest_in = tie((right, left, rest_in), w2)
        part = lambda k: [a[CHUNKS.index(k) * CHUNK :][:CHUNK] for a in (rest_m, rest_in)]
        to_right, to_left = part(3), part(5)
        to_right = jnp.concatenate(
            [add(right, *[a[:mid] for a in to_right]), add(*[a[mid:] for a in to_right])], axis=0
        )
        to_left = jnp.concatenate(
            [add(*[a[:mid] for a in to_left]), add(left, *[a[mid:] for a in to_left])], axis=0
        )
        right, left = ring(to_right, to_left)
        w1 = wgrad(1, pos, gt, *acts, to_right, to_left)
        w3 = wgrad(3, pos, gt, *acts, w1)
        up_y, down_y, sent = near_step(w1, w3, up_y, down_y, "y")
        right, left = tie((right, left), sent)
        to_right, to_left = add(right, *part(2)), add(left, *part(6))
        right, left = ring(to_right, to_left)
        w0 = wgrad(0, pos, gt, *acts, to_right, to_left)
        right, left = tie((right, left), w0)
        right, left = ring(add(right, *part(1)), add(left, *part(7)))
        row = add(right, left, *part(0))
    with jax.named_scope("input"):
        up_x, down_x = far_step(row[3 * STEP :], "x")
        up_x, down_x, _ = near_step(
            row[STEP : 2 * STEP], row[2 * STEP : 3 * STEP], up_x, down_x, "x"
        )
        own = add(row[:STEP], up_x, down_x)
        own, summed = tie((own, add(w0, up_y, down_y)))
        parts = [shift(summed[NX - r], "x", NX, -r) for r in (1, 2, 3)]
        col, parts = gather_eight(own, parts)
        input_grad = place(pos, col, shift(col, "c", NC, 1))
    with jax.named_scope("weight"):
        gate_grad, up_grad, down_grad = join(pos, [summed[0], *parts])
    return input_grad, gate_grad, up_grad, down_grad


def solution(mesh):
    grid = Mesh(mesh.devices.reshape(NY, NX, NZ, NC), ("y", "x", "z", "c"))
    dp, tensor = ("y", "x"), ("z", "c")
    return jax.shard_map(
        per_device,
        mesh=grid,
        in_specs=(P(dp, None), P(dp, None), P(dp, tensor), P(dp, tensor), P(tensor, dp)),
        out_specs=(P(dp, None), P(dp, tensor), P(dp, tensor), P(tensor, dp)),
        check_vma=False,
    )
```

```python
import functools

import jax
import jax.numpy as jnp
from jax import lax
from jax.experimental import pallas as pl
from jax.experimental.pallas import tpu as pltpu
from jax.sharding import Mesh, PartitionSpec as P

BF = jnp.bfloat16
F32 = jnp.float32
NY, NX, NZ, NC = 4, 4, 8, 2
TOK = 256
D = 4096
SHARE = 896
Q = SHARE // NX
DB = 256
ROWS = 3 * Q
HALF = D // 2
PARAMS = pltpu.CompilerParams(vmem_limit_bytes=56 * 1024 * 1024)
ANY = pl.BlockSpec(memory_space=pl.ANY)
VM = pl.BlockSpec(memory_space=pltpu.VMEM)
SM = pl.BlockSpec(memory_space=pltpu.SMEM)


def shift(value, axis, size, step):
    return lax.ppermute(value, axis, [(i, (i + step) % size) for i in range(size)])


def flip(value):
    return value.astype(BF).T


ORDER = (0, 1, 3, 2)
CHUNKS = (0, 1, 2, 3, 5, 6, 7, 4)
STEP = TOK // NZ
CHUNK = NX * STEP
BLOCKS = [(ry, rx) for ry in (2, 1, 3, 0) for rx in range(NX)]


def cut_kernel(pos, g_ref, u_ref, d_ref, o0, o1, o2, o3, gt, ut):
    gt[...] = flip(g_ref[...])
    ut[...] = flip(u_ref[...])
    x = pos[1]
    for r, o_ref in enumerate((o0, o1, o2, o3)):
        q0 = pl.multiple_of(lax.rem(x + r, NX) * Q, 16)
        o_ref[0:Q, :] = gt[pl.ds(q0, Q), :]
        o_ref[Q : 2 * Q, :] = ut[pl.ds(q0, Q), :]
        o_ref[2 * Q : ROWS, :] = d_ref[pl.ds(q0, Q), :]


def cut(pos, g, u, d):
    return pl.pallas_call(
        cut_kernel,
        out_shape=(jax.ShapeDtypeStruct((ROWS, DB), BF),) * NX,
        in_specs=[SM, VM, VM, VM],
        out_specs=(VM,) * NX,
        scratch_shapes=[pltpu.VMEM((SHARE, DB), BF), pltpu.VMEM((SHARE, DB), BF)],
        compiler_params=PARAMS,
        name="cut",
    )(pos, g, u, d)


def forward_kernel(places, pos, *refs):
    n = len(places)
    pieces = refs[:n]
    tok, cot, rest, near, far = refs[n : n + 5]
    outs, grads = refs[n + 5 : n + 9], refs[n + 9 : n + 16]
    wv, tv, cv, gt_ref, gg_ref, gz_ref, *held, wg, wsem, tsem, csem, osem = refs[n + 16 :]
    y, x, z, c = pos[0], pos[1], pos[2], pos[3]
    copies = []
    for ref, (ry, rx, count) in zip(pieces, places):
        for k in range(count):
            at = (lax.rem(y + ry, NY) * NX + lax.rem(x + rx + k, NX)) * DB
            copies.append(
                pltpu.make_async_copy(
                    ref if count == 1 else ref.at[k],
                    wv.at[:, pl.ds(pl.multiple_of(at, DB), DB)],
                    wsem.at[ry * NX + rx + k],
                )
            )
    tcopies, ccopies = [], []
    for slot, r in enumerate(ORDER):
        rows = pl.ds(slot * TOK, TOK)
        tcopies.append(
            pltpu.make_async_copy(tok if r == 0 else rest.at[r - 1], tv.at[rows], tsem.at[slot])
        )
        if r in (0, 2):
            src = cot if r == 0 else rest.at[3]
            ccopies.append([pltpu.make_async_copy(src, cv.at[rows], csem.at[slot, 0])])
        else:
            ccopies.append(
                [
                    pltpu.make_async_copy(
                        src.at[(r - 1) // 2],
                        cv.at[rows, pl.ds(pl.multiple_of(col * HALF, HALF), HALF)],
                        csem.at[slot, k],
                    )
                    for k, (src, col) in enumerate(((near, c), (far, 1 - c)))
                ]
            )

    def fetch(slot):
        tcopies[slot].start()
        for copy in ccopies[slot]:
            copy.start()

    for copy in copies:
        copy.start()
    fetch(0)
    for copy in copies:
        copy.wait()
    fetch(1)
    nt = (((1,), (1,)), ((), ()))
    for slot in range(NX):
        rows = slice(slot * TOK, (slot + 1) * TOK)
        if 1 <= slot < NX - 1:
            fetch(slot + 1)
        tcopies[slot].wait()
        gate = lax.dot_general(tv[rows], wv[0:Q, :], nt, preferred_element_type=F32)
        up = lax.dot_general(tv[rows], wv[Q : 2 * Q, :], nt, preferred_element_type=F32)
        for copy in ccopies[slot]:
            copy.wait()
        hidden_grad = lax.dot_general(
            cv[rows], wv[2 * Q : ROWS, :], nt, preferred_element_type=F32
        )
        s = jax.nn.sigmoid(gate)
        act = gate * s
        gate_grad = (hidden_grad * up * s * (1.0 + gate * (1.0 - s))).astype(BF)
        up_grad = (hidden_grad * act).astype(BF)
        gg_ref[rows, 0:Q] = gate_grad
        gg_ref[rows, Q : 2 * Q] = up_grad
        gt_ref[0:Q, rows] = gate_grad.T
        gt_ref[Q : 2 * Q, rows] = up_grad.T
        gt_ref[2 * Q : ROWS, rows] = flip(act * up)
    for i, k in enumerate(CHUNKS):
        for slot in range(NX):
            at = pl.multiple_of(slot * TOK + lax.rem(z + k, NZ) * STEP, STEP)
            gz_ref[(i * NX + slot) * STEP : (i * NX + slot + 1) * STEP, :] = gg_ref[
                pl.ds(at, STEP), :
            ]
    writes = []
    for k, half in enumerate((1 - c, c)):
        far_ref, rest_ref = held[2 * k : 2 * k + 2]
        for i in range(HALF // 512):
            cols = pl.ds(pl.multiple_of(half * HALF + i * 512, 512), 512)
            part = jnp.dot(gz_ref[...], wv[0 : 2 * Q, cols], preferred_element_type=F32).astype(BF)
            rest_ref[:, i * 512 : (i + 1) * 512] = part[0 : 7 * CHUNK]
            far_ref[:, i * 512 : (i + 1) * 512] = part[7 * CHUNK :]
        for m, ref in enumerate((far_ref, rest_ref)):
            writes.append(pltpu.make_async_copy(ref, outs[2 * k + m], osem.at[2 * k + m]))
            writes[-1].start()
    for i, (ry, rx) in enumerate(BLOCKS):
        at = (lax.rem(y + ry, NY) * NX + lax.rem(x + rx, NX)) * DB
        cols = pl.ds(pl.multiple_of(at, DB), DB)
        for rows, ref in ((slice(0, 2 * Q), tv), (slice(2 * Q, ROWS), cv)):
            wg[i, rows, :] = jnp.dot(
                gt_ref[rows, :], ref[:, cols], preferred_element_type=F32
            ).astype(BF)
        if i % 2 == 1 and i < 12 or i == 15:
            m = i // 2 if i < 12 else 6
            first = i - 1 if i < 12 else 12
            writes.append(
                pltpu.make_async_copy(
                    wg.at[pl.ds(first, i + 1 - first)], grads[m], osem.at[4 + m]
                )
            )
            writes[-1].start()
    for copy in writes:
        copy.wait()


def forward(pos, places, pieces, tok, cot, rest, near, far):
    parts = tuple(jax.ShapeDtypeStruct((k * CHUNK, HALF), BF) for k in (1, 7))
    grads = tuple(jax.ShapeDtypeStruct((k, ROWS, DB), BF) for k in (2,) * 6 + (4,))
    return pl.pallas_call(
        functools.partial(forward_kernel, places),
        out_shape=parts * 2 + grads,
        in_specs=[SM] + [ANY] * (len(pieces) + 5),
        out_specs=(ANY,) * 11,
        scratch_shapes=[
            pltpu.VMEM((ROWS, D), BF),
            pltpu.VMEM((NX * TOK, D), BF),
            pltpu.VMEM((NX * TOK, D), BF),
            pltpu.VMEM((ROWS, NX * TOK), BF),
            pltpu.VMEM((NX * TOK, 2 * Q), BF),
            pltpu.VMEM((NX * TOK, 2 * Q), BF),
            *[pltpu.VMEM(part.shape, BF) for part in parts * 2],
            pltpu.VMEM((NX * NY, ROWS, DB), BF),
            pltpu.SemaphoreType.DMA((NX * NY,)),
            pltpu.SemaphoreType.DMA((NX,)),
            pltpu.SemaphoreType.DMA((NX, 2)),
            pltpu.SemaphoreType.DMA((11,)),
        ],
        compiler_params=PARAMS,
        name="forward",
    )(pos, *pieces, tok, cot, rest, near, far)


def add(*parts):
    total = parts[0].astype(F32)
    for part in parts[1:]:
        total = total + part.astype(F32)
    return total.astype(BF)


def far_step(far, axis):
    mid = far.shape[0] // 2
    return shift(far[:mid], axis, 4, 1), shift(far[mid:], axis, 4, -1)


def near_step(after, before, up, down, axis):
    to_next = jnp.concatenate([add(after[0], up), after[1]], axis=0)
    to_prev = jnp.concatenate([before[0], add(before[1], down)], axis=0)
    return shift(to_next, axis, 4, 1), shift(to_prev, axis, 4, -1), (to_next, to_prev)


def tie(values, *others):
    return lax.optimization_barrier((values, others))[0]


def gather_eight(own, flying):
    mid = TOK // NZ // 2
    slots = {0: own}
    right = left = own
    for k in (1, 2, 3):
        right, left = shift(right, "z", NZ, 1), shift(left, "z", NZ, -1)
        slots[NZ - k], slots[k] = right, left
        if k == 3:
            right, left, flying = tie((right, left, flying))
    slots[4] = jnp.concatenate(
        [shift(right[:mid], "z", NZ, 1), shift(left[mid:], "z", NZ, -1)], axis=0
    )
    return jnp.stack([slots[k] for k in range(NZ)]), flying


def place_kernel(pos, a_ref, b_ref, o_ref):
    z, c = pos[2], pos[3]
    rows = TOK // NZ
    for k in range(NZ):
        at = pl.ds(pl.multiple_of(lax.rem(z + k, NZ) * rows, rows), rows)
        o_ref[at, pl.ds(pl.multiple_of(c * HALF, HALF), HALF)] = a_ref[k]
        o_ref[at, pl.ds(pl.multiple_of((1 - c) * HALF, HALF), HALF)] = b_ref[k]


def place(pos, mine, other):
    return pl.pallas_call(
        place_kernel,
        out_shape=jax.ShapeDtypeStruct((TOK, D), BF),
        in_specs=[SM, VM, VM],
        out_specs=VM,
        compiler_params=PARAMS,
        name="place",
    )(pos, mine, other)


def join_kernel(pos, a_ref, b_ref, c_ref, d_ref, g_ref, u_ref, o_ref, gt, ut):
    x = pos[1]
    for r, ref in enumerate((a_ref, b_ref, c_ref, d_ref)):
        at = pl.ds(pl.multiple_of(lax.rem(x + r, NX) * Q, 16), Q)
        gt[at, :] = ref[0:Q, :]
        ut[at, :] = ref[Q : 2 * Q, :]
        o_ref[at, :] = ref[2 * Q : ROWS, :]
    g_ref[...] = flip(gt[...])
    u_ref[...] = flip(ut[...])


def join(pos, parts):
    return pl.pallas_call(
        join_kernel,
        out_shape=(
            jax.ShapeDtypeStruct((DB, SHARE), BF),
            jax.ShapeDtypeStruct((DB, SHARE), BF),
            jax.ShapeDtypeStruct((SHARE, DB), BF),
        ),
        in_specs=[SM] + [VM] * 4,
        out_specs=(VM, VM, VM),
        scratch_shapes=[pltpu.VMEM((SHARE, DB), BF), pltpu.VMEM((SHARE, DB), BF)],
        compiler_params=PARAMS,
        name="join",
    )(pos, *parts)


def per_device(tokens, cotangent, gate_weight, up_weight, down_weight):
    y, x, z, c = (lax.axis_index(a).astype(jnp.int32) for a in ("y", "x", "z", "c"))
    pos = jnp.stack([y, x, z, c])
    with jax.named_scope("weights"):
        cuts = cut(pos, gate_weight, up_weight, down_weight)
        mine = [shift(cuts[NX - r], "x", NX, -r) for r in (1, 3)]
    with jax.named_scope("tokens"):
        start = (z * NC + c) * (TOK // (NZ * NC))
        own = tie((tokens, cotangent), cuts)
        seed_t, seed_c = (
            lax.dynamic_slice_in_dim(a, start, TOK // (NZ * NC), 0)[None] for a in own
        )
        two = shift(jnp.concatenate([seed_t, seed_c]), "x", NX, 2)
        seeds = [shift(seed_t, "x", NX, -1), two[:1], shift(seed_t, "x", NX, 1), two[1:]]
        seeds, mine, cuts = tie((jnp.concatenate(seeds), mine, cuts))
        rest = lax.all_gather(seeds, ("z", "c"), axis=1, tiled=True)
    with jax.named_scope("weights"):
        mine.insert(1, shift(cuts[2], "x", NX, 2))
        above0, below0 = shift(cuts[0], "y", NY, -1), shift(cuts[0], "y", NY, 1)
    half = lax.dynamic_slice_in_dim(cotangent, c * HALF, HALF, 1)
    mine, above0, below0, half = tie((mine, above0, below0, half))
    with jax.named_scope("weights"):
        slab = jnp.stack(mine)
        above, below = shift(slab, "y", NY, -1), shift(slab, "y", NY, 1)
    with jax.named_scope("tokens"):
        from_next, from_prev = shift(half, "x", NX, -1), shift(half, "x", NX, 1)
    above, below, from_next, from_prev = tie((above, below, from_next, from_prev))
    with jax.named_scope("weights"):
        across01 = shift(jnp.stack([above0, above[0]]), "y", NY, -1)
        across23 = shift(below[1:], "y", NY, 1)
        pieces = [cuts[0], *mine, above0, above, below0, below, across01, across23]
        places = [(0, 0, 1), (0, 1, 1), (0, 2, 1), (0, 3, 1)]
        places += [(1, 0, 1), (1, 1, 3), (3, 0, 1), (3, 1, 3), (2, 0, 2), (2, 2, 2)]
    with jax.named_scope("tokens"):
        near = jnp.stack([from_next, from_prev])
        far = shift(near, "c", NC, 1)
    acts = (tokens, cotangent, rest, near, far)
    with jax.named_scope("forward"):
        far_o, rest_o, far_m, rest_m, *grads = forward(pos, places, pieces, *acts)
    ring = lambda a, b: (shift(a, "z", NZ, 1), shift(b, "z", NZ, -1))
    with jax.named_scope("grads"):
        far_in = shift(far_o, "c", NC, 1)
        far, mid = add(far_m, far_in), CHUNK // 2
        rest_in = shift(tie(rest_o, far_in), "c", NC, 1)
        right, left = ring(far[:mid], far[mid:])
        up_y, down_y = shift(grads[0], "y", NY, 1), shift(grads[1], "y", NY, -1)
        w0 = grads[6]
        part = lambda k: [a[CHUNKS.index(k) * CHUNK :][:CHUNK] for a in (rest_m, rest_in)]
        to_right, to_left = part(3), part(5)
        to_right = jnp.concatenate(
            [add(right, *[a[:mid] for a in to_right]), add(*[a[mid:] for a in to_right])], axis=0
        )
        to_left = jnp.concatenate(
            [add(*[a[:mid] for a in to_left]), add(left, *[a[mid:] for a in to_left])], axis=0
        )
        right, left = ring(to_right, to_left)
        up_y, down_y, sent = near_step(
            grads[2:4], grads[4:6], *tie((up_y, down_y), (to_right, to_left)), "y"
        )
        right, left = tie((right, left), sent)
        to_right, to_left = add(right, *part(2)), add(left, *part(6))
        right, left = ring(to_right, to_left)
        right, left = ring(add(right, *part(1)), add(left, *part(7)))
        right, left, summed = tie((right, left, add(w0, up_y, down_y)))
        row = add(right, left, *part(0))
        parts = [shift(summed[NX - r], "x", NX, -r) for r in (1, 2, 3)]
    with jax.named_scope("input"):
        pieces = [row[i * STEP : (i + 1) * STEP] for i in range(NX)]
        own = add(pieces[0], *[shift(v, "x", NX, r) for v, r in zip(pieces[1:], ORDER[1:])])
        col, parts = gather_eight(own, parts)
        input_grad = place(pos, col, shift(col, "c", NC, 1))
    with jax.named_scope("weight"):
        gate_grad, up_grad, down_grad = join(pos, [summed[0], *parts])
    return input_grad, gate_grad, up_grad, down_grad


def solution(mesh):
    grid = Mesh(mesh.devices.reshape(NY, NX, NZ, NC), ("y", "x", "z", "c"))
    dp, tensor = ("y", "x"), ("z", "c")
    return jax.shard_map(
        per_device,
        mesh=grid,
        in_specs=(P(dp, None), P(dp, None), P(dp, tensor), P(dp, tensor), P(tensor, dp)),
        out_specs=(P(dp, None), P(dp, tensor), P(dp, tensor), P(tensor, dp)),
        check_vma=False,
    )
```

```python
import functools

import jax
import jax.numpy as jnp
from jax import lax
from jax.experimental import pallas as pl
from jax.experimental.pallas import tpu as pltpu
from jax.sharding import Mesh, PartitionSpec as P

BF = jnp.bfloat16
F32 = jnp.float32
NY, NX, NZ, NC = 4, 4, 8, 2
TOK = 256
D = 4096
SHARE = 896
Q = SHARE // NX
DB = 256
ROWS = 3 * Q
HALF = D // 2
PARAMS = pltpu.CompilerParams(vmem_limit_bytes=56 * 1024 * 1024)
ANY = pl.BlockSpec(memory_space=pl.ANY)
VM = pl.BlockSpec(memory_space=pltpu.VMEM)
SM = pl.BlockSpec(memory_space=pltpu.SMEM)


def shift(value, axis, size, step):
    return lax.ppermute(value, axis, [(i, (i + step) % size) for i in range(size)])


def flip(value):
    return value.astype(BF).T


ORDER = (0, 1, 3, 2)
CHUNKS = (0, 1, 2, 3, 5, 6, 7, 4)
STEP = TOK // NZ
CHUNK = NX * STEP
SEED = TOK // (NZ * NC)
BLOCKS = [(ry, rx) for ry in (2, 1, 3, 0) for rx in range(NX)]


def cut_kernel(pos, g_ref, u_ref, d_ref, tok, cot, o0, o1, o2, o3, one, both, gt, ut, sems):
    rows = pl.ds(pl.multiple_of((pos[2] * NC + pos[3]) * SEED, SEED), SEED)
    copies = [
        pltpu.make_async_copy(src.at[rows], dst, sems.at[i])
        for i, (src, dst) in enumerate(((tok, one.at[0]), (tok, both.at[0]), (cot, both.at[1])))
    ]
    for copy in copies:
        copy.start()
    gt[...] = flip(g_ref[...])
    ut[...] = flip(u_ref[...])
    x = pos[1]
    for r, o_ref in enumerate((o0, o1, o2, o3)):
        q0 = pl.multiple_of(lax.rem(x + r, NX) * Q, 16)
        o_ref[0:Q, :] = gt[pl.ds(q0, Q), :]
        o_ref[Q : 2 * Q, :] = ut[pl.ds(q0, Q), :]
        o_ref[2 * Q : ROWS, :] = d_ref[pl.ds(q0, Q), :]
    for copy in copies:
        copy.wait()


def cut(pos, g, u, d, tok, cot):
    return pl.pallas_call(
        cut_kernel,
        out_shape=(jax.ShapeDtypeStruct((ROWS, DB), BF),) * NX
        + tuple(jax.ShapeDtypeStruct((k, SEED, D), BF) for k in (1, 2)),
        in_specs=[SM, VM, VM, VM, ANY, ANY],
        out_specs=(VM,) * (NX + 2),
        scratch_shapes=[
            pltpu.VMEM((SHARE, DB), BF),
            pltpu.VMEM((SHARE, DB), BF),
            pltpu.SemaphoreType.DMA((3,)),
        ],
        compiler_params=PARAMS,
        name="cut",
    )(pos, g, u, d, tok, cot)


def forward_kernel(places, pos, *refs):
    n = len(places)
    pieces = refs[:n]
    tok, cot, rest, near, far = refs[n : n + 5]
    outs, grads = refs[n + 5 : n + 9], refs[n + 9]
    wv, tv, cv, gt_ref, gg_ref, gz_ref, *held, wg, wsem, tsem, csem, osem = refs[n + 10 :]
    y, x, z, c = pos[0], pos[1], pos[2], pos[3]
    copies = []
    for ref, (ry, rx, count) in zip(pieces, places):
        for k in range(count):
            at = (lax.rem(y + ry, NY) * NX + lax.rem(x + rx + k, NX)) * DB
            copies.append(
                pltpu.make_async_copy(
                    ref if count == 1 else ref.at[k],
                    wv.at[:, pl.ds(pl.multiple_of(at, DB), DB)],
                    wsem.at[ry * NX + rx + k],
                )
            )
    tcopies, ccopies = [], []
    for slot, r in enumerate(ORDER):
        rows = pl.ds(slot * TOK, TOK)
        tcopies.append(
            pltpu.make_async_copy(tok if r == 0 else rest.at[r - 1], tv.at[rows], tsem.at[slot])
        )
        if r in (0, 2):
            src = cot if r == 0 else rest.at[3]
            ccopies.append([pltpu.make_async_copy(src, cv.at[rows], csem.at[slot, 0])])
        else:
            ccopies.append(
                [
                    pltpu.make_async_copy(
                        src.at[(r - 1) // 2],
                        cv.at[rows, pl.ds(pl.multiple_of(col * HALF, HALF), HALF)],
                        csem.at[slot, k],
                    )
                    for k, (src, col) in enumerate(((near, c), (far, 1 - c)))
                ]
            )

    def fetch(slot):
        tcopies[slot].start()
        for copy in ccopies[slot]:
            copy.start()

    for copy in copies:
        copy.start()
    fetch(0)
    for copy in copies:
        copy.wait()
    fetch(1)
    nt = (((1,), (1,)), ((), ()))
    for slot in range(NX):
        rows = slice(slot * TOK, (slot + 1) * TOK)
        if 1 <= slot < NX - 1:
            fetch(slot + 1)
        tcopies[slot].wait()
        gate = lax.dot_general(tv[rows], wv[0:Q, :], nt, preferred_element_type=F32)
        up = lax.dot_general(tv[rows], wv[Q : 2 * Q, :], nt, preferred_element_type=F32)
        for copy in ccopies[slot]:
            copy.wait()
        hidden_grad = lax.dot_general(
            cv[rows], wv[2 * Q : ROWS, :], nt, preferred_element_type=F32
        )
        s = jax.nn.sigmoid(gate)
        act = gate * s
        gate_grad = (hidden_grad * up * s * (1.0 + gate * (1.0 - s))).astype(BF)
        up_grad = (hidden_grad * act).astype(BF)
        gg_ref[rows, 0:Q] = gate_grad
        gg_ref[rows, Q : 2 * Q] = up_grad
        gt_ref[0:Q, rows] = gate_grad.T
        gt_ref[Q : 2 * Q, rows] = up_grad.T
        gt_ref[2 * Q : ROWS, rows] = flip(act * up)
    for i, k in enumerate(CHUNKS):
        for slot in range(NX):
            at = pl.multiple_of(slot * TOK + lax.rem(z + k, NZ) * STEP, STEP)
            gz_ref[(i * NX + slot) * STEP : (i * NX + slot + 1) * STEP, :] = gg_ref[
                pl.ds(at, STEP), :
            ]
    writes = []
    for k, half in enumerate((1 - c, c)):
        far_ref, rest_ref = held[2 * k : 2 * k + 2]
        for i in range(HALF // 512):
            cols = pl.ds(pl.multiple_of(half * HALF + i * 512, 512), 512)
            part = jnp.dot(gz_ref[...], wv[0 : 2 * Q, cols], preferred_element_type=F32).astype(BF)
            into = slice(i % 2 * 512, (i % 2 + 1) * 512)
            rest_ref[i // 2, :, into] = part[0 : 7 * CHUNK]
            far_ref[i // 2, :, into] = part[7 * CHUNK :]
        for m, ref in enumerate((far_ref, rest_ref)):
            writes.append(pltpu.make_async_copy(ref, outs[2 * k + m], osem.at[2 * k + m]))
            writes[-1].start()
    for i, ry in enumerate((2, 1, 3, 0)):

        @pl.loop(0, NX, unroll=2)
        def _(rx):
            at = (lax.rem(y + ry, NY) * NX + lax.rem(x + rx, NX)) * DB
            cols = pl.ds(pl.multiple_of(at, DB), DB)
            for rows, ref in ((slice(0, 2 * Q), tv), (slice(2 * Q, ROWS), cv)):
                wg[i * NX + rx, rows, :] = jnp.dot(
                    gt_ref[rows, :], ref[:, cols], preferred_element_type=F32
                ).astype(BF)

        writes.append(
            pltpu.make_async_copy(
                wg.at[pl.ds(i * NX, NX)], grads.at[lax.rem(y + ry, NY)], osem.at[4 + ry]
            )
        )
        writes[-1].start()
    for copy in writes:
        copy.wait()


def forward(pos, places, pieces, tok, cot, rest, near, far):
    parts = tuple(jax.ShapeDtypeStruct((2, k * CHUNK, HALF // 2), BF) for k in (1, 7))
    grads = jax.ShapeDtypeStruct((NY, NX, ROWS, DB), BF)
    return pl.pallas_call(
        functools.partial(forward_kernel, places),
        out_shape=parts * 2 + (grads,),
        in_specs=[SM] + [ANY] * (len(pieces) + 5),
        out_specs=(ANY,) * 5,
        scratch_shapes=[
            pltpu.VMEM((ROWS, D), BF),
            pltpu.VMEM((NX * TOK, D), BF),
            pltpu.VMEM((NX * TOK, D), BF),
            pltpu.VMEM((ROWS, NX * TOK), BF),
            pltpu.VMEM((NX * TOK, 2 * Q), BF),
            pltpu.VMEM((NX * TOK, 2 * Q), BF),
            *[pltpu.VMEM(part.shape, BF) for part in parts * 2],
            pltpu.VMEM((NX * NY, ROWS, DB), BF),
            pltpu.SemaphoreType.DMA((NX * NY,)),
            pltpu.SemaphoreType.DMA((NX,)),
            pltpu.SemaphoreType.DMA((NX, 2)),
            pltpu.SemaphoreType.DMA((8,)),
        ],
        compiler_params=PARAMS,
        name="forward",
    )(pos, *pieces, tok, cot, rest, near, far)


def add(*parts):
    total = parts[0].astype(F32)
    for part in parts[1:]:
        total = total + part.astype(F32)
    return total.astype(BF)


def tie(values, *others):
    return lax.optimization_barrier((values, others))[0]


def gather_eight(own, flying):
    mid = TOK // NZ // 2
    slots = {0: own}
    right = left = own
    for k in (1, 2, 3):
        right, left = shift(right, "z", NZ, 1), shift(left, "z", NZ, -1)
        slots[NZ - k], slots[k] = right, left
        if k == 3:
            right, left, flying = tie((right, left, flying))
    slots[4] = jnp.concatenate(
        [shift(right[:mid], "z", NZ, 1), shift(left[mid:], "z", NZ, -1)], axis=0
    )
    return jnp.stack([slots[k] for k in range(NZ)]), flying


def place_kernel(pos, a_ref, b_ref, o_ref):
    z, c = pos[2], pos[3]
    rows = TOK // NZ
    for k in range(NZ):
        at = pl.ds(pl.multiple_of(lax.rem(z + k, NZ) * rows, rows), rows)
        o_ref[at, pl.ds(pl.multiple_of(c * HALF, HALF), HALF)] = a_ref[k]
        o_ref[at, pl.ds(pl.multiple_of((1 - c) * HALF, HALF), HALF)] = b_ref[k]


def place(pos, mine, other):
    return pl.pallas_call(
        place_kernel,
        out_shape=jax.ShapeDtypeStruct((TOK, D), BF),
        in_specs=[SM, VM, VM],
        out_specs=VM,
        compiler_params=PARAMS,
        name="place",
    )(pos, mine, other)


def join_kernel(pos, a_ref, b_ref, c_ref, d_ref, g_ref, u_ref, o_ref, gt, ut):
    x = pos[1]
    for r, ref in enumerate((a_ref, b_ref, c_ref, d_ref)):
        at = pl.ds(pl.multiple_of(lax.rem(x + r, NX) * Q, 16), Q)
        gt[at, :] = ref[0:Q, :]
        ut[at, :] = ref[Q : 2 * Q, :]
        o_ref[at, :] = ref[2 * Q : ROWS, :]
    g_ref[...] = flip(gt[...])
    u_ref[...] = flip(ut[...])


def join(pos, parts):
    return pl.pallas_call(
        join_kernel,
        out_shape=(
            jax.ShapeDtypeStruct((DB, SHARE), BF),
            jax.ShapeDtypeStruct((DB, SHARE), BF),
            jax.ShapeDtypeStruct((SHARE, DB), BF),
        ),
        in_specs=[SM] + [VM] * 4,
        out_specs=(VM, VM, VM),
        scratch_shapes=[pltpu.VMEM((SHARE, DB), BF), pltpu.VMEM((SHARE, DB), BF)],
        compiler_params=PARAMS,
        name="join",
    )(pos, *parts)


def per_device(tokens, cotangent, gate_weight, up_weight, down_weight):
    y, x, z, c = (lax.axis_index(a).astype(jnp.int32) for a in ("y", "x", "z", "c"))
    pos = jnp.stack([y, x, z, c])
    with jax.named_scope("weights"):
        *cuts, seed, both = cut(
            pos, gate_weight, up_weight, down_weight, tokens, cotangent
        )
        mine = [shift(cuts[NX - r], "x", NX, -r) for r in (1, 3)]
    with jax.named_scope("tokens"):
        two = shift(both, "x", NX, 2)
        seeds = [shift(seed, "x", NX, -1), two[:1], shift(seed, "x", NX, 1), two[1:]]
        seeds, mine, cuts = tie((jnp.concatenate(seeds), mine, cuts))
        rest = lax.all_gather(seeds, ("z", "c"), axis=1, tiled=True)
    with jax.named_scope("weights"):
        mine.insert(1, shift(cuts[2], "x", NX, 2))
        above0, below0 = shift(cuts[0], "y", NY, -1), shift(cuts[0], "y", NY, 1)
    half = lax.dynamic_slice_in_dim(cotangent, c * HALF, HALF, 1)
    mine, above0, below0, half = tie((mine, above0, below0, half))
    with jax.named_scope("weights"):
        slab = jnp.stack(mine)
        above, below = shift(slab, "y", NY, -1), shift(slab, "y", NY, 1)
    with jax.named_scope("tokens"):
        from_next, from_prev = shift(half, "x", NX, -1), shift(half, "x", NX, 1)
    above, below, from_next, from_prev = tie((above, below, from_next, from_prev))
    with jax.named_scope("weights"):
        across01 = shift(jnp.stack([above0, above[0]]), "y", NY, -1)
        across23 = shift(below[1:], "y", NY, 1)
        pieces = [cuts[0], *mine, above0, above, below0, below, across01, across23]
        places = [(0, 0, 1), (0, 1, 1), (0, 2, 1), (0, 3, 1)]
        places += [(1, 0, 1), (1, 1, 3), (3, 0, 1), (3, 1, 3), (2, 0, 2), (2, 2, 2)]
    with jax.named_scope("tokens"):
        near = jnp.stack([from_next, from_prev])
        far = shift(near, "c", NC, 1)
    acts = (tokens, cotangent, rest, near, far)
    with jax.named_scope("forward"):
        far_o, rest_o, far_m, rest_m, grads = forward(pos, places, pieces, *acts)
    ring = lambda a, b: (shift(a, "z", NZ, 1), shift(b, "z", NZ, -1))
    with jax.named_scope("weight"):
        summed = lax.psum_scatter(grads, "y", scatter_dimension=0, tiled=True)[0]
    with jax.named_scope("input"):
        far_in = shift(far_o, "c", NC, 1)
        far, mid = add(far_m, far_in), CHUNK // 2
        rest_in = shift(tie(rest_o, far_in), "c", NC, 1)
        flows = [ring(far[q, :mid], far[q, mid:]) for q in range(2)]
        part = lambda q, k: [
            a[q, CHUNKS.index(k) * CHUNK :][:CHUNK] for a in (rest_m, rest_in)
        ]
        sent = far
        for k in (3, 2, 1):
            for q in range(2):
                right, left = tie(flows[q], sent)
                to_right, to_left = part(q, k), part(q, NZ - k)
                if k == 3:
                    right = [add(right, *[a[:mid] for a in to_right]), add(*[a[mid:] for a in to_right])]
                    left = [add(*[a[:mid] for a in to_left]), add(left, *[a[mid:] for a in to_left])]
                    sent = jnp.concatenate(right, axis=0), jnp.concatenate(left, axis=0)
                else:
                    sent = add(right, *to_right), add(left, *to_left)
                flows[q] = ring(*sent)
        row = jnp.concatenate([add(*flows[q], *part(q, 0)) for q in range(2)], axis=1)
        pieces = [row[i * STEP : (i + 1) * STEP] for i in range(NX)]
        own = add(pieces[0], *[shift(v, "x", NX, r) for v, r in zip(pieces[1:], ORDER[1:])])
        own, summed = tie((own, summed))
        parts = [shift(summed[NX - r], "x", NX, -r) for r in (1, 2, 3)]
        col, parts = gather_eight(own, parts)
        input_grad = place(pos, col, shift(col, "c", NC, 1))
    with jax.named_scope("weight"):
        gate_grad, up_grad, down_grad = join(pos, [summed[0], *parts])
    return input_grad, gate_grad, up_grad, down_grad


def solution(mesh):
    grid = Mesh(mesh.devices.reshape(NY, NX, NZ, NC), ("y", "x", "z", "c"))
    dp, tensor = ("y", "x"), ("z", "c")
    return jax.shard_map(
        per_device,
        mesh=grid,
        in_specs=(P(dp, None), P(dp, None), P(dp, tensor), P(dp, tensor), P(tensor, dp)),
        out_specs=(P(dp, None), P(dp, tensor), P(dp, tensor), P(tensor, dp)),
        check_vma=False,
    )
```

```python
import functools

import jax
import jax.numpy as jnp
from jax import lax
from jax.experimental import pallas as pl
from jax.experimental.pallas import tpu as pltpu
from jax.sharding import Mesh, PartitionSpec as P

BF = jnp.bfloat16
F32 = jnp.float32
NY, NX, NZ, NC = 4, 4, 8, 2
TOK = 256
D = 4096
SHARE = 896
Q = SHARE // NX
DB = 256
ROWS = 3 * Q
HALF = D // 2
PARAMS = pltpu.CompilerParams(vmem_limit_bytes=56 * 1024 * 1024)
ANY = pl.BlockSpec(memory_space=pl.ANY)
VM = pl.BlockSpec(memory_space=pltpu.VMEM)
SM = pl.BlockSpec(memory_space=pltpu.SMEM)


def shift(value, axis, size, step):
    return lax.ppermute(value, axis, [(i, (i + step) % size) for i in range(size)])


def flip(value):
    return value.astype(BF).T


ORDER = (0, 1, 3, 2)
CHUNKS = (0, 1, 2, 3, 5, 6, 7, 4)
STEP = TOK // NZ
CHUNK = NX * STEP
SEED = TOK // (NZ * NC)
BLOCKS = [(ry, rx) for ry in (2, 1, 3, 0) for rx in range(NX)]


def cut_kernel(pos, g_ref, u_ref, d_ref, tok, cot, o0, o1, o2, o3, one, both, gt, ut, sems):
    rows = pl.ds(pl.multiple_of((pos[2] * NC + pos[3]) * SEED, SEED), SEED)
    copies = [
        pltpu.make_async_copy(src.at[rows], dst, sems.at[i])
        for i, (src, dst) in enumerate(((tok, one.at[0]), (tok, both.at[0]), (cot, both.at[1])))
    ]
    for copy in copies:
        copy.start()
    gt[...] = flip(g_ref[...])
    ut[...] = flip(u_ref[...])
    x = pos[1]
    for r, o_ref in enumerate((o0, o1, o2, o3)):
        q0 = pl.multiple_of(lax.rem(x + r, NX) * Q, 16)
        o_ref[0:Q, :] = gt[pl.ds(q0, Q), :]
        o_ref[Q : 2 * Q, :] = ut[pl.ds(q0, Q), :]
        o_ref[2 * Q : ROWS, :] = d_ref[pl.ds(q0, Q), :]
    for copy in copies:
        copy.wait()


def cut(pos, g, u, d, tok, cot):
    return pl.pallas_call(
        cut_kernel,
        out_shape=(jax.ShapeDtypeStruct((ROWS, DB), BF),) * NX
        + tuple(jax.ShapeDtypeStruct((k, SEED, D), BF) for k in (1, 2)),
        in_specs=[SM, VM, VM, VM, ANY, ANY],
        out_specs=(VM,) * (NX + 2),
        scratch_shapes=[
            pltpu.VMEM((SHARE, DB), BF),
            pltpu.VMEM((SHARE, DB), BF),
            pltpu.SemaphoreType.DMA((3,)),
        ],
        compiler_params=PARAMS,
        name="cut",
    )(pos, g, u, d, tok, cot)


def forward_kernel(places, pos, *refs):
    n = len(places)
    pieces = refs[:n]
    tok, cot, rest, near, far = refs[n : n + 5]
    outs, grads = refs[n + 5 : n + 9], refs[n + 9]
    wv, tv, cv, gt_ref, gg_ref, gz_ref, *held, wg, wsem, tsem, csem, osem = refs[n + 10 :]
    y, x, z, c = pos[0], pos[1], pos[2], pos[3]
    copies = []
    for ref, (ry, rx, count) in zip(pieces, places):
        for k in range(count):
            at = (lax.rem(y + ry, NY) * NX + lax.rem(x + rx + k, NX)) * DB
            copies.append(
                pltpu.make_async_copy(
                    ref if count == 1 else ref.at[k],
                    wv.at[:, pl.ds(pl.multiple_of(at, DB), DB)],
                    wsem.at[ry * NX + rx + k],
                )
            )
    tcopies, ccopies = [], []
    for slot, r in enumerate(ORDER):
        rows = pl.ds(slot * TOK, TOK)
        tcopies.append(
            pltpu.make_async_copy(tok if r == 0 else rest.at[r - 1], tv.at[rows], tsem.at[slot])
        )
        if r in (0, 2):
            src = cot if r == 0 else rest.at[3]
            ccopies.append([pltpu.make_async_copy(src, cv.at[rows], csem.at[slot, 0])])
        else:
            ccopies.append(
                [
                    pltpu.make_async_copy(
                        src.at[(r - 1) // 2],
                        cv.at[rows, pl.ds(pl.multiple_of(col * HALF, HALF), HALF)],
                        csem.at[slot, k],
                    )
                    for k, (src, col) in enumerate(((near, c), (far, 1 - c)))
                ]
            )

    def fetch(slot):
        tcopies[slot].start()
        for copy in ccopies[slot]:
            copy.start()

    for copy in copies:
        copy.start()
    fetch(0)
    for copy in copies:
        copy.wait()
    fetch(1)
    nt = (((1,), (1,)), ((), ()))

    def products(slot):
        rows = slice(slot * TOK, (slot + 1) * TOK)
        if 1 <= slot < NX - 1:
            fetch(slot + 1)
        tcopies[slot].wait()
        for copy in ccopies[slot]:
            copy.wait()
        return [
            lax.dot_general(
                act[rows], wv[m * Q : (m + 1) * Q, :], nt, preferred_element_type=F32
            )
            for m, act in enumerate((tv, tv, cv))
        ]

    def gradients(slot, gate, up, hidden_grad):
        rows = slice(slot * TOK, (slot + 1) * TOK)
        s = jax.nn.sigmoid(gate)
        act = gate * s
        gate_grad = (hidden_grad * up * s * (1.0 + gate * (1.0 - s))).astype(BF)
        up_grad = (hidden_grad * act).astype(BF)
        gg_ref[rows, 0:Q] = gate_grad
        gg_ref[rows, Q : 2 * Q] = up_grad
        gt_ref[0:Q, rows] = gate_grad.T
        gt_ref[Q : 2 * Q, rows] = up_grad.T
        gt_ref[2 * Q : ROWS, rows] = flip(act * up)

    ahead = products(0)
    for slot in range(NX):
        now, ahead = ahead, products(slot + 1) if slot < NX - 1 else None
        gradients(slot, *now)
    for i, k in enumerate(CHUNKS):
        for slot in range(NX):
            at = pl.multiple_of(slot * TOK + lax.rem(z + k, NZ) * STEP, STEP)
            gz_ref[(i * NX + slot) * STEP : (i * NX + slot + 1) * STEP, :] = gg_ref[
                pl.ds(at, STEP), :
            ]
    writes = []
    for k, half in enumerate((1 - c, c)):
        far_ref, rest_ref = held[2 * k : 2 * k + 2]
        for i in range(HALF // 512):
            cols = pl.ds(pl.multiple_of(half * HALF + i * 512, 512), 512)
            part = jnp.dot(gz_ref[...], wv[0 : 2 * Q, cols], preferred_element_type=F32).astype(BF)
            into = slice(i % 2 * 512, (i % 2 + 1) * 512)
            rest_ref[i // 2, :, into] = part[0 : 7 * CHUNK]
            far_ref[i // 2, :, into] = part[7 * CHUNK :]
        for m, ref in enumerate((far_ref, rest_ref)):
            writes.append(pltpu.make_async_copy(ref, outs[2 * k + m], osem.at[2 * k + m]))
            writes[-1].start()
    for i, ry in enumerate((2, 1, 3, 0)):

        @pl.loop(0, NX, unroll=2)
        def _(rx):
            at = (lax.rem(y + ry, NY) * NX + lax.rem(x + rx, NX)) * DB
            cols = pl.ds(pl.multiple_of(at, DB), DB)
            for rows, ref in ((slice(0, 2 * Q), tv), (slice(2 * Q, ROWS), cv)):
                wg[i * NX + rx, rows, :] = jnp.dot(
                    gt_ref[rows, :], ref[:, cols], preferred_element_type=F32
                ).astype(BF)

        writes.append(
            pltpu.make_async_copy(
                wg.at[pl.ds(i * NX, NX)], grads.at[lax.rem(y + ry, NY)], osem.at[4 + ry]
            )
        )
        writes[-1].start()
    for copy in writes:
        copy.wait()


def forward(pos, places, pieces, tok, cot, rest, near, far):
    parts = tuple(jax.ShapeDtypeStruct((2, k * CHUNK, HALF // 2), BF) for k in (1, 7))
    grads = jax.ShapeDtypeStruct((NY, NX, ROWS, DB), BF)
    return pl.pallas_call(
        functools.partial(forward_kernel, places),
        out_shape=parts * 2 + (grads,),
        in_specs=[SM] + [ANY] * (len(pieces) + 5),
        out_specs=(ANY,) * 5,
        scratch_shapes=[
            pltpu.VMEM((ROWS, D), BF),
            pltpu.VMEM((NX * TOK, D), BF),
            pltpu.VMEM((NX * TOK, D), BF),
            pltpu.VMEM((ROWS, NX * TOK), BF),
            pltpu.VMEM((NX * TOK, 2 * Q), BF),
            pltpu.VMEM((NX * TOK, 2 * Q), BF),
            *[pltpu.VMEM(part.shape, BF) for part in parts * 2],
            pltpu.VMEM((NX * NY, ROWS, DB), BF),
            pltpu.SemaphoreType.DMA((NX * NY,)),
            pltpu.SemaphoreType.DMA((NX,)),
            pltpu.SemaphoreType.DMA((NX, 2)),
            pltpu.SemaphoreType.DMA((8,)),
        ],
        compiler_params=PARAMS,
        name="forward",
    )(pos, *pieces, tok, cot, rest, near, far)


def add(*parts):
    total = parts[0].astype(F32)
    for part in parts[1:]:
        total = total + part.astype(F32)
    return total.astype(BF)


def tie(values, *others):
    return lax.optimization_barrier((values, others))[0]


def gather_eight(own, flying):
    mid = TOK // NZ // 2
    slots = {0: own}
    right = left = own
    for k in (1, 2, 3):
        right, left = shift(right, "z", NZ, 1), shift(left, "z", NZ, -1)
        slots[NZ - k], slots[k] = right, left
        if k == 3:
            right, left, flying = tie((right, left, flying))
    slots[4] = jnp.concatenate(
        [shift(right[:mid], "z", NZ, 1), shift(left[mid:], "z", NZ, -1)], axis=0
    )
    return jnp.stack([slots[k] for k in range(NZ)]), flying


def place_kernel(pos, a_ref, b_ref, o_ref):
    z, c = pos[2], pos[3]
    rows = TOK // NZ
    for k in range(NZ):
        at = pl.ds(pl.multiple_of(lax.rem(z + k, NZ) * rows, rows), rows)
        o_ref[at, pl.ds(pl.multiple_of(c * HALF, HALF), HALF)] = a_ref[k]
        o_ref[at, pl.ds(pl.multiple_of((1 - c) * HALF, HALF), HALF)] = b_ref[k]


def place(pos, mine, other):
    return pl.pallas_call(
        place_kernel,
        out_shape=jax.ShapeDtypeStruct((TOK, D), BF),
        in_specs=[SM, VM, VM],
        out_specs=VM,
        compiler_params=PARAMS,
        name="place",
    )(pos, mine, other)


def join_kernel(pos, a_ref, b_ref, c_ref, d_ref, g_ref, u_ref, o_ref, gt, ut):
    x = pos[1]
    for r, ref in enumerate((a_ref, b_ref, c_ref, d_ref)):
        at = pl.ds(pl.multiple_of(lax.rem(x + r, NX) * Q, 16), Q)
        gt[at, :] = ref[0:Q, :]
        ut[at, :] = ref[Q : 2 * Q, :]
        o_ref[at, :] = ref[2 * Q : ROWS, :]
    g_ref[...] = flip(gt[...])
    u_ref[...] = flip(ut[...])


def join(pos, parts):
    return pl.pallas_call(
        join_kernel,
        out_shape=(
            jax.ShapeDtypeStruct((DB, SHARE), BF),
            jax.ShapeDtypeStruct((DB, SHARE), BF),
            jax.ShapeDtypeStruct((SHARE, DB), BF),
        ),
        in_specs=[SM] + [VM] * 4,
        out_specs=(VM, VM, VM),
        scratch_shapes=[pltpu.VMEM((SHARE, DB), BF), pltpu.VMEM((SHARE, DB), BF)],
        compiler_params=PARAMS,
        name="join",
    )(pos, *parts)


def per_device(tokens, cotangent, gate_weight, up_weight, down_weight):
    y, x, z, c = (lax.axis_index(a).astype(jnp.int32) for a in ("y", "x", "z", "c"))
    pos = jnp.stack([y, x, z, c])
    with jax.named_scope("weights"):
        *cuts, seed, both = cut(
            pos, gate_weight, up_weight, down_weight, tokens, cotangent
        )
        mine = [shift(cuts[NX - r], "x", NX, -r) for r in (1, 3)]
    with jax.named_scope("tokens"):
        two = shift(both, "x", NX, 2)
        seeds = [shift(seed, "x", NX, -1), two[:1], shift(seed, "x", NX, 1), two[1:]]
        seeds, mine, cuts = tie((jnp.concatenate(seeds), mine, cuts))
        rest = lax.all_gather(seeds, ("z", "c"), axis=1, tiled=True)
    with jax.named_scope("weights"):
        mine.insert(1, shift(cuts[2], "x", NX, 2))
        above0, below0 = shift(cuts[0], "y", NY, -1), shift(cuts[0], "y", NY, 1)
    half = lax.dynamic_slice_in_dim(cotangent, c * HALF, HALF, 1)
    mine, above0, below0, half = tie((mine, above0, below0, half))
    with jax.named_scope("weights"):
        slab = jnp.stack(mine)
        above, below = shift(slab, "y", NY, -1), shift(slab, "y", NY, 1)
    with jax.named_scope("tokens"):
        from_next, from_prev = shift(half, "x", NX, -1), shift(half, "x", NX, 1)
    above, below, from_next, from_prev = tie((above, below, from_next, from_prev))
    with jax.named_scope("weights"):
        across01 = shift(jnp.stack([above0, above[0]]), "y", NY, -1)
        across23 = shift(below[1:], "y", NY, 1)
        pieces = [cuts[0], *mine, above0, above, below0, below, across01, across23]
        places = [(0, 0, 1), (0, 1, 1), (0, 2, 1), (0, 3, 1)]
        places += [(1, 0, 1), (1, 1, 3), (3, 0, 1), (3, 1, 3), (2, 0, 2), (2, 2, 2)]
    with jax.named_scope("tokens"):
        near = jnp.stack([from_next, from_prev])
        far = shift(near, "c", NC, 1)
    acts = (tokens, cotangent, rest, near, far)
    with jax.named_scope("forward"):
        far_o, rest_o, far_m, rest_m, grads = forward(pos, places, pieces, *acts)
    ring = lambda a, b: (shift(a, "z", NZ, 1), shift(b, "z", NZ, -1))
    with jax.named_scope("weight"):
        summed = lax.psum_scatter(grads, "y", scatter_dimension=0, tiled=True)[0]
    with jax.named_scope("input"):
        far_in = shift(far_o, "c", NC, 1)
        far, mid = add(far_m, far_in), CHUNK // 2
        rest_in = shift(tie(rest_o, far_in), "c", NC, 1)
        flows = [ring(far[q, :mid], far[q, mid:]) for q in range(2)]
        part = lambda q, k: [
            a[q, CHUNKS.index(k) * CHUNK :][:CHUNK] for a in (rest_m, rest_in)
        ]
        sent = far
        for k in (3, 2, 1):
            for q in range(2):
                right, left = tie(flows[q], sent)
                to_right, to_left = part(q, k), part(q, NZ - k)
                if k == 3:
                    right = [add(right, *[a[:mid] for a in to_right]), add(*[a[mid:] for a in to_right])]
                    left = [add(*[a[:mid] for a in to_left]), add(left, *[a[mid:] for a in to_left])]
                    sent = jnp.concatenate(right, axis=0), jnp.concatenate(left, axis=0)
                else:
                    sent = add(right, *to_right), add(left, *to_left)
                flows[q] = ring(*sent)
        row = jnp.concatenate([add(*flows[q], *part(q, 0)) for q in range(2)], axis=1)
        pieces = [row[i * STEP : (i + 1) * STEP] for i in range(NX)]
        own = add(pieces[0], *[shift(v, "x", NX, r) for v, r in zip(pieces[1:], ORDER[1:])])
        own, summed = tie((own, summed))
        parts = [shift(summed[NX - r], "x", NX, -r) for r in (1, 2, 3)]
        col, parts = gather_eight(own, parts)
        input_grad = place(pos, col, shift(col, "c", NC, 1))
    with jax.named_scope("weight"):
        gate_grad, up_grad, down_grad = join(pos, [summed[0], *parts])
    return input_grad, gate_grad, up_grad, down_grad


def solution(mesh):
    grid = Mesh(mesh.devices.reshape(NY, NX, NZ, NC), ("y", "x", "z", "c"))
    dp, tensor = ("y", "x"), ("z", "c")
    return jax.shard_map(
        per_device,
        mesh=grid,
        in_specs=(P(dp, None), P(dp, None), P(dp, tensor), P(dp, tensor), P(tensor, dp)),
        out_specs=(P(dp, None), P(dp, tensor), P(dp, tensor), P(tensor, dp)),
        check_vma=False,
    )
```
